512 devices in a mesh: outer: 32 (over z, core), inner: 16 (over y, x).
Axes of the slice: x: 4, y: 4, z: 16, core: 2. Of those that a mesh axis runs over, the one named last changes fastest.
Arguments:
- tokens: bfloat16 [4096, 4096], P('outer', 'inner'), may hold values from -6 to 6
- routes: int32 [4096, 8], P('outer'), may hold values from 0 to 127, all different within a row; in each aligned block of 128 rows (0 to 127, 128 to 255, ...) at most 10 rows name the same one
- gates: float32 [4096, 8], P('outer'), may hold values from 0.1 to 1
- w_gate_up: bfloat16 [128, 4096, 1536], P('outer', 'inner'), may hold values from -0.09375 to 0.09375
- w_down: bfloat16 [128, 768, 4096], P('outer', None, 'inner'), may hold values from -0.21875 to 0.21875
Outputs:
- mixed: bfloat16 [4096, 4096], P('outer', 'inner')
The draws below stay inside these ranges and needn't reach their ends.
Inputs may be any that keep to these rules, and one draw needn't show every extreme that they name: `routes`: each row names 8 different experts; within each aligned block of 128 rows no expert is named more than 10 times, a bound that some block reaches.
All inputs are finite; a program needn't handle non-finite values.
Results may differ from the reference program's by a relative error of at most 0.024.
Values may be sent and summed in bfloat16 or wider, within the bound.
No kernel may reach another device: no remote copies, remote signals or barrier semaphores. Data moves between devices by JAX's collectives and lax.ppermute only.
A program may use at most 64 MiB of HBM per device.

```python
import math
import jax
import jax.numpy as jnp
import numpy as np
from jax import lax

D = 4096
H = 768
TOPK = 8
TOK_DEV = 128
EXPERTS = 128
CAP = 10
TOKENS = 4096
N_OUTER = 32
N_INNER = 16


def block_scale(rng, extent, split, low, largest):
    level, own = 1.0, jax.random.fold_in(rng, 6)
    for position, shards_of in split:
        draws = jnp.exp(jax.random.uniform(jax.random.fold_in(own, position), (shards_of,), jnp.float32, low / len(split), largest / len(split)))
        level = level * jnp.repeat(draws, extent[position] // shards_of).reshape([-1 if axis == position else 1 for axis in range(len(extent))])
    return level


def routed_block(rng, own, number, rows, number_of, top, bound, skew):
    order = jax.random.permutation(rng, number_of)
    crowded, common = load_shares(number_of, rows * top, bound, skew, True), load_shares(number_of, rows * top, bound, skew, False)
    places = jnp.arange(number_of)

    def named(lengths, rotation):
        used = int((lengths > 0).sum())
        fixed = max(1, used // 4)
        passed = fixed + (places - fixed + rotation * (used - fixed)) % max(1, number_of - fixed)
        return jnp.zeros((number_of,), jnp.int32).at[order[jnp.where(places < fixed, places, passed)]].set(jnp.asarray(lengths, jnp.int32))

    lengths = jnp.where(number % 4 == 0, named(crowded, number // 4), named(common, number - number // 4 - 1))
    mixed = jax.random.permutation(jax.random.fold_in(own, 3), number_of)
    giver, taker = mixed[0:number_of // 2 * 2:2], mixed[1:number_of // 2 * 2:2]
    margin = jnp.minimum(lengths[giver] - 1, bound - lengths[taker]) // 2
    margin = jnp.where((giver == order[0]) | (taker == order[0]) | (lengths[taker] == 0), 0, jnp.maximum(margin, 0))
    passed = jax.random.randint(jax.random.fold_in(own, 4), (number_of // 2,), 0, 1 << 20) % (margin + 1)
    lengths = lengths.at[giver].add(-passed).at[taker].add(passed)
    items = jnp.searchsorted(jnp.cumsum(lengths), jnp.arange(rows * top), side="right").astype(jnp.int32)
    grid = items.reshape(top, rows).T
    grid = grid[jax.random.permutation(jax.random.fold_in(own, 1), rows)]
    rotation = jax.random.randint(jax.random.fold_in(own, 2), (rows, 1), 0, top)
    return jnp.take_along_axis(grid, (jnp.arange(top)[None, :] + rotation) % top, axis=1)


def load_shares(number_of, total, limit, lean, full):
    portions = [(1 << 20) // math.isqrt(rank ** lean) + 1 for rank in range(1, number_of + 1)]
    largest = limit if full else min(limit, max(-(-total // number_of), total * portions[0] // sum(portions)))
    least = 1 if total - largest >= number_of - 1 else 0
    given, rest = [largest] + [least] * (number_of - 1), total - largest - least * (number_of - 1)
    while rest > 0:
        candidates = [i for i in range(1, number_of) if given[i] < largest] or [i for i in range(1, number_of) if given[i] < limit]
        whole, left = sum([portions[i] for i in candidates]), rest
        for i in candidates:
            extra = min(limit - given[i], max(1, left * portions[i] // whole), rest)
            given[i] = given[i] + extra
            rest = rest - extra
    return np.array(given)


def centred(stream_key, shape, spread, reach, shards=(), kind=jnp.bfloat16):
    values = spread * jax.random.normal(stream_key, shape, jnp.float32)
    if shards:
        values = values * block_scale(stream_key, shape, shards, -0.22, 0.18)
    return jnp.clip(values, -reach, reach).astype(kind)


def setup_inputs(seed: int = 0) -> dict:
    streams_of = jax.random.split(jax.random.key(seed), 6)
    tokens = centred(streams_of[0], (TOKENS, D), 1.0, 6.0, ((0, 32), (1, 16)))
    routes_keys = jax.random.split(jax.random.fold_in(streams_of[1], 1), TOKENS // TOK_DEV)
    routes_turns = jax.random.permutation(jax.random.fold_in(streams_of[1], 3), TOKENS // TOK_DEV)
    routes = jax.vmap(lambda own, number: routed_block(jax.random.fold_in(streams_of[1], 2), own, number, TOK_DEV, EXPERTS, TOPK, CAP, 2))(routes_keys, routes_turns).reshape((TOKENS, TOPK))
    gates = jnp.clip(0.1 + 0.9 * jax.random.uniform(streams_of[2], (TOKENS, TOPK), jnp.float32) ** block_scale(streams_of[2], (TOKENS, TOPK), ((0, 32),), -0.2, 0.2), 0.1, 1.0)
    w_gate_up = centred(streams_of[3], (EXPERTS, D, 2 * H), D ** -0.5, 0.09375, ((0, 32), (1, 16)))
    w_down = centred(streams_of[4], (EXPERTS, H, D), H ** -0.5, 0.21875, ((0, 32), (2, 16)))
    return dict(tokens=tokens, routes=routes, gates=gates, w_gate_up=w_gate_up, w_down=w_down)


def reference(tokens, routes, gates, w_gate_up, w_down):
    experts = EXPERTS
    slot_count = N_OUTER * CAP
    route_count = TOKENS * TOPK
    feature_share = D // N_INNER
    hidden_share = H // N_INNER
    flat_ids = routes.reshape(-1).astype(jnp.int32)
    owners = (jnp.arange(route_count, dtype=jnp.int32) // TOPK).astype(jnp.int32)
    onehot = (flat_ids[:, None] == jnp.arange(experts, dtype=jnp.int32)[None, :]).astype(jnp.int32)
    slot_rank = jnp.sum((jnp.cumsum(onehot, axis=0) - 1) * onehot, axis=1).astype(jnp.int32)
    slot_rows = jnp.zeros((experts, slot_count), jnp.int32).at[flat_ids, slot_rank].set(owners)
    slot_gates = jnp.zeros((experts, slot_count), jnp.float32).at[flat_ids, slot_rank].set(gates.reshape(-1))

    def one_expert(summed, expert_item):
        rows_index, weights_row, w_in, w_out = expert_item
        chosen = tokens[rows_index].astype(jnp.float32).reshape(slot_count, N_INNER, feature_share)
        w_blocks = w_in.astype(jnp.float32).reshape(N_INNER, feature_share, 2 * H)
        partial_value = jnp.einsum("snd,ndh->nsh", chosen, w_blocks)
        partial_value = lax.optimization_barrier(partial_value.astype(jnp.bfloat16)).astype(jnp.float32)
        gate_up = jnp.sum(partial_value, axis=0).reshape(slot_count, N_INNER, 2, hidden_share)
        hidden = (jax.nn.silu(gate_up[:, :, 0]) * gate_up[:, :, 1]).reshape(slot_count, H).astype(jnp.bfloat16)
        result = jnp.dot(hidden, w_out, preferred_element_type=jnp.float32).astype(jnp.bfloat16)
        summed = summed.at[rows_index].add(weights_row[:, None] * result.astype(jnp.float32))
        return summed, None

    summed, _ = lax.scan(one_expert, jnp.zeros((TOKENS, D), jnp.float32), (slot_rows, slot_gates, w_gate_up, w_down))
    return (tokens.astype(jnp.float32) + summed).astype(jnp.bfloat16)
```

```python
import functools

import jax
import jax.numpy as jnp
from jax import lax
from jax.experimental import pallas as pl
from jax.experimental.pallas import tpu as pltpu
from jax.sharding import PartitionSpec as P

F32 = jnp.float32
BF16 = jnp.bfloat16
VMEM_LIMIT = 40 * 1024 * 1024


def iota(shape, dim):
    return lax.broadcasted_iota(jnp.int32, shape, dim)


def tenth(value):
    return (value * 6554) >> 16


def dot(a, b, contract=((1,), (0,))):
    return lax.dot_general(a, b, (contract, ((), ())), preferred_element_type=F32)


def slot_codes(routes_ref, experts):
    rows, top = routes_ref.shape
    expert = iota((rows, experts), 1)
    named = jnp.zeros((rows, experts), F32)
    for k in range(top):
        named = named + jnp.where(routes_ref[:, k : k + 1] == expert, 1.0, 0.0)
    earlier = jnp.where(iota((rows, rows), 1) < iota((rows, rows), 0), 1.0, 0.0).astype(BF16)
    rank = dot(earlier, named.astype(BF16))
    return (named * (rank + 1.0)).astype(BF16)


def pack_kernel(cap, experts, routes_ref, tokens_ref, packed_ref):
    rows = tokens_ref.shape[0]
    slots = experts * cap
    code = slot_codes(routes_ref, experts)
    slot = iota((slots, experts), 0)
    spread = jnp.where(tenth(slot) == iota((slots, experts), 1), 1.0, 0.0).astype(BF16)
    seen = dot(spread, code, ((1,), (1,)))
    slot = iota((slots, rows), 0)
    wanted = (slot - cap * tenth(slot) + 1).astype(F32)
    placing = jnp.where(seen == wanted, 1.0, 0.0).astype(BF16)
    packed_ref[...] = dot(placing, tokens_ref[...]).astype(BF16)


def gate_kernel(cap, experts, routes_ref, gates_ref, weights_ref):
    rows, top = routes_ref.shape
    slots = experts * cap
    code = slot_codes(routes_ref, experts)
    expert = iota((rows, experts), 1)
    gate = jnp.zeros((rows, experts), F32)
    for k in range(top):
        gate = gate + jnp.where(routes_ref[:, k : k + 1] == expert, gates_ref[:, k : k + 1], 0.0)
    slot = iota((experts, slots), 1)
    spread = jnp.where(tenth(slot) == iota((experts, slots), 0), 1.0, 0.0).astype(BF16)
    slot = iota((rows, slots), 1)
    mine = dot(code, spread) == (slot - cap * tenth(slot) + 1).astype(F32)
    for part in range(weights_ref.shape[0]):
        piece = gate.astype(BF16)
        gate = gate - piece.astype(F32)
        weights_ref[part] = jnp.where(mine, dot(piece, spread), 0.0).astype(BF16)


def pair_slots(cap, group, per_expert, pair, shape, dim):
    lane = iota(shape, dim)
    second = jnp.where(lane >= per_expert, 1, 0)
    lane = lane - per_expert * second
    source = tenth(lane)
    return source * (group * cap) + (2 * pair + second) * cap + (lane - cap * source)


def up_kernel(cap, group, per_expert, arrived_ref, w_ref, out_ref, slab_ref):
    pair, column = pl.program_id(0), pl.program_id(1)
    slots = arrived_ref.shape[0]
    both = 2 * per_expert
    mid = per_expert // 128 * 128

    @pl.when(column == 0)
    def _():
        source = pair_slots(cap, group, per_expert, pair, (both, slots), 0)
        order = jnp.where(source == iota((both, slots), 1), 1.0, 0.0).astype(BF16)
        slab_ref[...] = dot(order, arrived_ref[...]).astype(BF16)

    first = dot(w_ref[0], slab_ref[: mid + 128, :], ((0,), (1,)))
    second = dot(w_ref[1], slab_ref[mid:, :], ((0,), (1,)))
    lane = iota((first.shape[0], 128), 1)
    out_ref[:, :mid] = first[:, :mid].astype(BF16)
    out_ref[:, mid : mid + 128] = jnp.where(
        lane < per_expert - mid, first[:, mid:], second[:, :128]
    ).astype(BF16)
    out_ref[:, mid + 128 :] = second[:, 128:].astype(BF16)


def sum_kernel(parts_ref, out_ref):
    total = parts_ref[0].astype(F32)
    for n in range(1, parts_ref.shape[0]):
        total = total + parts_ref[n].astype(F32)
    out_ref[...] = total.astype(BF16)


def hidden_kernel(parts_ref, out_ref):
    total = parts_ref[0].astype(F32)
    for n in range(1, parts_ref.shape[0]):
        total = total + parts_ref[n].astype(F32)
    share = total.shape[0] // 2
    gate, up = total[:share], total[share:]
    hidden = (gate / (1.0 + jnp.exp(-gate)) * up).astype(BF16)
    for n in range(out_ref.shape[0]):
        out_ref[n] = hidden


def down_kernel(cap, group, per_expert, hidden_ref, w_ref, out_ref, total_ref):
    pair = pl.program_id(0)
    slots = out_ref.shape[0]
    both = 2 * per_expert
    mid = per_expert // 128 * 128
    first = dot(hidden_ref[:, : mid + 128], w_ref[0], ((0,), (0,))).astype(BF16)
    second = dot(hidden_ref[:, mid:], w_ref[1], ((0,), (0,))).astype(BF16)
    rows = jnp.concatenate([first[:per_expert], second[per_expert - mid :]], axis=0)
    source = pair_slots(cap, group, per_expert, pair, (slots, both), 1)
    order = jnp.where(source == iota((slots, both), 0), 1.0, 0.0).astype(BF16)
    placed = dot(order, rows)

    @pl.when(pair == 0)
    def _():
        total_ref[...] = placed

    @pl.when(pair == pl.num_programs(0) - 1)
    def _():
        out_ref[...] = (total_ref[...] + placed).astype(BF16)


def mix_kernel(tokens_ref, weights_ref, home_ref, out_ref):
    total = tokens_ref[...].astype(F32)
    home = home_ref[...]
    for part in range(weights_ref.shape[0]):
        total = total + dot(weights_ref[part], home)
    out_ref[...] = total.astype(BF16)


def params(*semantics):
    return pltpu.CompilerParams(
        dimension_semantics=semantics or None, vmem_limit_bytes=VMEM_LIMIT
    )


def cost(flops, nbytes):
    return pl.CostEstimate(flops=flops, bytes_accessed=nbytes, transcendentals=0)


def groups_of(outer, side):
    along, across, whole = [], [], []
    for o in range(outer):
        square = [[o * side * side + y * side + x for x in range(side)] for y in range(side)]
        turned = [list(line) for line in zip(*square)]
        if o % 2 == 0:
            square, turned = turned, square
        along += turned
        across += square
        whole.append([device for line in square for device in line])
    return along, across, whole


def per_device(mesh_shape, tokens, routes, gates, w_gate_up, w_down):
    rows, features = tokens.shape
    outer, inner = mesh_shape
    group, _, columns = w_gate_up.shape
    hidden = w_down.shape[1]
    experts = group * outer
    cap = 10
    slots = experts * cap
    per_expert = outer * cap
    side = 4
    axes = ("outer", "inner")
    along, across, whole = groups_of(outer, side)

    packed = pl.pallas_call(
        functools.partial(pack_kernel, cap, experts),
        out_shape=jax.ShapeDtypeStruct((slots, features), BF16),
        compiler_params=params(),
        cost_estimate=cost(2 * slots * rows * 384, 2 * slots * features),
        name="pack",
    )(routes, tokens)
    arrived = lax.all_to_all(packed, "outer", split_axis=0, concat_axis=0, tiled=True)

    tile = columns // side
    partial_value = pl.pallas_call(
        functools.partial(up_kernel, cap, group, per_expert),
        grid=(group // 2, columns // tile),
        in_specs=[
            pl.BlockSpec((slots, features), lambda p, c: (0, 0)),
            pl.BlockSpec((2, features, tile), lambda p, c: (p, 0, c)),
        ],
        out_specs=pl.BlockSpec((tile, 2 * per_expert), lambda p, c: (c, p)),
        out_shape=jax.ShapeDtypeStruct((columns, slots), BF16),
        scratch_shapes=[pltpu.VMEM((2 * per_expert, features), BF16)],
        compiler_params=params("arbitrary", "arbitrary"),
        cost_estimate=cost(2 * slots * features * (columns + slots), 2 * columns * slots),
        name="gate_up",
    )(arrived, w_gate_up)

    swapped = lax.all_to_all(
        partial_value, axes, split_axis=0, concat_axis=0, tiled=True, axis_index_groups=along
    )
    quarter = columns // side
    lanes = 256
    summed = pl.pallas_call(
        sum_kernel,
        grid=(slots // lanes,),
        in_specs=[pl.BlockSpec((side, quarter, lanes), lambda n: (0, 0, n))],
        out_specs=pl.BlockSpec((quarter, lanes), lambda n: (0, n)),
        out_shape=jax.ShapeDtypeStruct((quarter, slots), BF16),
        compiler_params=params("arbitrary"),
        cost_estimate=cost(columns * slots, 2 * columns * slots),
        name="first_sum",
    )(swapped.reshape(side, quarter, slots))
    swapped = lax.all_to_all(
        summed, axes, split_axis=0, concat_axis=0, tiled=True, axis_index_groups=across
    )
    share = columns // inner
    mine = pl.pallas_call(
        hidden_kernel,
        grid=(slots // lanes,),
        in_specs=[pl.BlockSpec((side, share, lanes), lambda n: (0, 0, n))],
        out_specs=pl.BlockSpec((inner, share // 2, lanes), lambda n: (0, 0, n)),
        out_shape=jax.ShapeDtypeStruct((inner, share // 2, slots), BF16),
        compiler_params=params("arbitrary"),
        cost_estimate=cost(quarter * slots, 4 * quarter * slots),
        name="hidden",
    )(swapped.reshape(side, share, slots))
    gathered = lax.all_to_all(
        mine.reshape(hidden, slots),
        axes,
        split_axis=0,
        concat_axis=0,
        tiled=True,
        axis_index_groups=whole,
    )
    expert_out = pl.pallas_call(
        functools.partial(down_kernel, cap, group, per_expert),
        grid=(group // 2,),
        in_specs=[
            pl.BlockSpec((hidden, 2 * per_expert), lambda p: (0, p)),
            pl.BlockSpec((2, hidden, features), lambda p: (p, 0, 0)),
        ],
        out_specs=pl.BlockSpec((slots, features), lambda p: (0, 0)),
        out_shape=jax.ShapeDtypeStruct((slots, features), BF16),
        scratch_shapes=[pltpu.VMEM((slots, features), F32)],
        compiler_params=params("arbitrary"),
        cost_estimate=cost(2 * slots * features * (hidden + slots), 4 * hidden * slots),
        name="down",
    )(gathered, w_down)
    weights = pl.pallas_call(
        functools.partial(gate_kernel, cap, experts),
        out_shape=jax.ShapeDtypeStruct((3, rows, slots), BF16),
        compiler_params=params(),
        cost_estimate=cost(8 * rows * experts * slots, 6 * rows * slots),
        name="gate_weights",
    )(routes, gates)
    home = lax.all_to_all(expert_out, "outer", split_axis=0, concat_axis=0, tiled=True)
    return pl.pallas_call(
        mix_kernel,
        out_shape=jax.ShapeDtypeStruct((rows, features), BF16),
        compiler_params=params(),
        cost_estimate=cost(6 * rows * slots * features, 2 * slots * features),
        name="mix",
    )(tokens, weights, home)


def solution(mesh):
    in_specs = (
        P("outer", "inner"),
        P("outer", None),
        P("outer", None),
        P("outer", "inner", None),
        P("outer", None, "inner"),
    )
    return jax.shard_map(
        functools.partial(per_device, (mesh.shape["outer"], mesh.shape["inner"])),
        mesh=mesh,
        in_specs=in_specs,
        out_specs=P("outer", "inner"),
        check_vma=False,
    )
```

```python
import functools

import jax
import jax.numpy as jnp
from jax import lax
from jax.experimental import pallas as pl
from jax.experimental.pallas import tpu as pltpu
from jax.sharding import PartitionSpec as P

F32 = jnp.float32
BF16 = jnp.bfloat16
VMEM_LIMIT = 40 * 1024 * 1024


def iota(shape, dim):
    return lax.broadcasted_iota(jnp.int32, shape, dim)


def tenth(value):
    return (value * 6554) >> 16


def dot(a, b, contract=((1,), (0,))):
    return lax.dot_general(a, b, (contract, ((), ())), preferred_element_type=F32)


def slot_codes(named):
    rows = named.shape[1]
    earlier = jnp.where(iota((rows, rows), 0) < iota((rows, rows), 1), 1.0, 0.0).astype(BF16)
    rank = dot(named.astype(BF16), earlier)
    return named * (rank + 1.0)


def pack_kernel(cap, experts, routes_ref, tokens_ref, packed_ref):
    top, rows = routes_ref.shape
    slots = experts * cap
    expert = iota((experts, rows), 0)
    named = jnp.zeros((experts, rows), F32)
    for k in range(top):
        named = named + jnp.where(routes_ref[k : k + 1, :] == expert, 1.0, 0.0)
    code = slot_codes(named).astype(BF16)
    slot = iota((slots, 1), 0)
    spread = jnp.where(tenth(slot) == iota((slots, experts), 1), 1.0, 0.0).astype(BF16)
    wanted = (slot - cap * tenth(slot) + 1).astype(F32)
    placing = jnp.where(dot(spread, code) == wanted, 1.0, 0.0).astype(BF16)
    packed_ref[...] = dot(placing, tokens_ref[...]).astype(BF16)


def gate_kernel(cap, experts, routes_ref, gates_ref, weights_ref):
    top, rows = routes_ref.shape
    slots = experts * cap
    expert = iota((experts, rows), 0)
    named = jnp.zeros((experts, rows), F32)
    gate = jnp.zeros((experts, rows), F32)
    for k in range(top):
        here = routes_ref[k : k + 1, :] == expert
        named = named + jnp.where(here, 1.0, 0.0)
        gate = gate + jnp.where(here, gates_ref[k : k + 1, :], 0.0)
    code = slot_codes(named).T.astype(BF16)
    gate = gate.T
    slot = iota((1, slots), 1)
    spread = jnp.where(tenth(slot) == iota((experts, slots), 0), 1.0, 0.0).astype(BF16)
    mine = dot(code, spread) == (slot - cap * tenth(slot) + 1).astype(F32)
    for part in range(weights_ref.shape[0]):
        piece = gate.astype(BF16)
        gate = gate - piece.astype(F32)
        weights_ref[part] = jnp.where(mine, dot(piece, spread), 0.0).astype(BF16)


def expert_order(cap, group, sources, shape, dim):
    row = iota(shape, dim)
    piece = tenth(row)
    expert = jnp.zeros_like(piece)
    for n in range(1, group):
        expert = expert + jnp.where(piece >= n * sources, 1, 0)
    source = piece - sources * expert
    return source * (group * cap) + expert * cap + (row - cap * piece)


def to_experts_kernel(cap, group, sources, rows_ref, out_ref):
    batch = sources * group * cap
    each = sources * cap
    place = expert_order(cap, group, sources, (batch, 1), 0)
    order = jnp.where(place == iota((batch, batch), 1), 1.0, 0.0).astype(BF16)
    for n in range(rows_ref.shape[0] // batch):
        moved = dot(order, rows_ref[n * batch : (n + 1) * batch, :]).astype(BF16)
        for e in range(group):
            out_ref[e, n * each : (n + 1) * each, :] = moved[e * each : (e + 1) * each]


def to_sources_kernel(cap, group, sources, rows_ref, out_ref):
    batch = sources * group * cap
    each = sources * cap
    place = expert_order(cap, group, sources, (1, batch), 1)
    order = jnp.where(place == iota((batch, batch), 0), 1.0, 0.0).astype(BF16)
    for n in range(out_ref.shape[0] // batch):
        rows = jnp.concatenate(
            [rows_ref[e, n * each : (n + 1) * each, :] for e in range(group)], axis=0
        )
        out_ref[n * batch : (n + 1) * batch, :] = dot(order, rows).astype(BF16)


def up_kernel(me_ref, rows_ref, own_ref, *refs):
    others, out_ref = refs[:-1], refs[-1]
    side = rows_ref.shape[0]
    tile = out_ref.shape[2]
    total = dot(rows_ref[me_ref[0]], own_ref[0])
    for k, w_ref in enumerate(others, 1):
        total = total + dot(rows_ref[lax.rem(me_ref[0] + side - k, side)], w_ref[...])
    for n in range(out_ref.shape[0]):
        out_ref[n] = total[:, n * tile : (n + 1) * tile].astype(BF16)


def hidden_kernel(share, parts_ref, out_ref):
    total = parts_ref[0].astype(F32)
    for n in range(1, parts_ref.shape[0]):
        total = total + parts_ref[n].astype(F32)
    width = total.shape[1]
    up = pltpu.roll(total, width - share, 1)
    mixed = (total / (1.0 + jnp.exp(-total)) * up).astype(BF16)
    column = iota((width, 1), 0)
    block = jnp.zeros_like(column)
    for n in range(1, width // (2 * share)):
        block = block + jnp.where(column >= 2 * share * n, 1, 0)
    unit = jnp.where(column - 2 * share * block < share, column - share * block, -width)
    lane = iota((width, width), 1)
    left = jnp.where(unit == lane, 1.0, 0.0).astype(BF16)
    right = jnp.where(unit + width // 2 == lane, 1.0, 0.0).astype(BF16)
    half = total.shape[0] // 2
    hidden = (dot(mixed[:half], left) + dot(mixed[half:], right)).astype(BF16)
    for n in range(out_ref.shape[0]):
        out_ref[n] = hidden


def down_kernel(batches, me_ref, hidden_ref, own_ref, *refs):
    others, out_ref = refs[:-1], refs[-1]
    side, packed, width = hidden_ref.shape
    half = packed // batches
    left = jnp.concatenate([hidden_ref[b, :, : width // 2] for b in range(side)], axis=1)
    right = jnp.concatenate([hidden_ref[b, :, width // 2 :] for b in range(side)], axis=1)
    pieces = []
    for n in range(batches):
        pieces += [left[n * half : (n + 1) * half], right[n * half : (n + 1) * half]]
    hidden = jnp.concatenate(pieces, axis=0)
    out_ref[me_ref[0]] = dot(hidden, own_ref[0]).astype(BF16)
    features = out_ref.shape[2]
    for k, w_ref in enumerate(others, 1):
        depth = w_ref.shape[0]
        total = None
        for n in range(hidden.shape[1] // depth):
            w = w_ref[:, n * features : (n + 1) * features]
            term = dot(hidden[:, n * depth : (n + 1) * depth], w)
            total = term if total is None else total + term
        out_ref[lax.rem(me_ref[0] + side - k, side)] = total.astype(BF16)


def mix_kernel(tokens_ref, weights_ref, home_ref, out_ref):
    total = tokens_ref[...].astype(F32)
    home = home_ref[...]
    for part in range(weights_ref.shape[0]):
        total = total + dot(weights_ref[part], home)
    out_ref[...] = total.astype(BF16)


def params(*semantics):
    return pltpu.CompilerParams(
        dimension_semantics=semantics or None, vmem_limit_bytes=VMEM_LIMIT
    )


def cost(flops, nbytes):
    return pl.CostEstimate(flops=flops, bytes_accessed=nbytes, transcendentals=0)


def lines_of(outer, side):
    along, across = [], []
    for o in range(outer):
        rows = [[o * side * side + y * side + x for x in range(side)] for y in range(side)]
        columns = [list(line) for line in zip(*rows)]
        along += columns if o % 2 == 0 else rows
        across += rows if o % 2 == 0 else columns
    return along, across


def per_device(mesh_shape, tokens, routes, gates, w_gate_up, w_down):
    rows, features = tokens.shape
    outer, inner = mesh_shape
    group, _, columns = w_gate_up.shape
    hidden = w_down.shape[1]
    experts = group * outer
    cap = 10
    slots = experts * cap
    per_expert = outer * cap
    side = group
    sources = 8
    axes = ("outer", "inner")
    along, across = lines_of(outer, side)
    square = lax.axis_index("inner")
    me = jnp.where(lax.axis_index("outer") % 2 == 0, square // side, square % side)
    me_ref = me.astype(jnp.int32).reshape(1)

    def exchange(value, lines):
        return lax.all_to_all(
            value, axes, split_axis=0, concat_axis=0, tiled=True, axis_index_groups=lines
        )

    def take(weights, k):
        return lax.dynamic_index_in_dim(weights, (me + k) % side, 0, keepdims=False)

    line_weights = []
    for k in range(1, side):
        pairs = [(line[n], line[(n + k) % side]) for line in along for n in range(side)]
        down = take(w_down, k)
        blocks = [down[n : n + features] for n in range(0, hidden, features)]
        moved = jnp.concatenate([take(w_gate_up, k), *blocks], axis=1)
        line_weights.append(lax.ppermute(moved, axes, pairs))
    routes, gates = routes.T, gates.T

    packed = pl.pallas_call(
        functools.partial(pack_kernel, cap, experts),
        out_shape=jax.ShapeDtypeStruct((slots, features), BF16),
        compiler_params=params(),
        cost_estimate=cost(2 * slots * rows * 384, 2 * slots * features),
        name="pack",
    )(routes, tokens)
    arrived = lax.all_to_all(packed, "outer", split_axis=0, concat_axis=0, tiled=True)
    by_expert = pl.pallas_call(
        functools.partial(to_experts_kernel, cap, group, sources),
        out_shape=jax.ShapeDtypeStruct((group, per_expert, features), BF16),
        compiler_params=params(),
        cost_estimate=cost(2 * slots * features * 320, 4 * slots * features),
        name="to_experts",
    )(arrived)
    by_expert = exchange(by_expert.reshape(slots, features), along)

    tile = columns // side
    partial_value = pl.pallas_call(
        up_kernel,
        grid_spec=pltpu.PrefetchScalarGridSpec(
            num_scalar_prefetch=1,
            grid=(side // 2,),
            in_specs=[
                pl.BlockSpec((side, per_expert, features), lambda c, me: (0, 0, 0)),
                pl.BlockSpec((1, features, 2 * tile), lambda c, me: (me[0], 0, c)),
            ]
            + [pl.BlockSpec((features, 2 * tile), lambda c, me: (0, c))] * (side - 1),
            out_specs=pl.BlockSpec((2, per_expert, tile), lambda c, me: (c, 0, 0)),
        ),
        out_shape=jax.ShapeDtypeStruct((side, per_expert, tile), BF16),
        compiler_params=params("arbitrary"),
        cost_estimate=cost(2 * slots * features * columns, 8 * features * columns),
        name="gate_up",
    )(me_ref, by_expert.reshape(side, per_expert, features), w_gate_up, *line_weights)
    swapped = exchange(partial_value.reshape(side * per_expert, tile), across)
    batches = 2
    packed_rows = per_expert // 2
    mine = pl.pallas_call(
        functools.partial(hidden_kernel, hidden // inner),
        grid=(batches,),
        in_specs=[pl.BlockSpec((side, per_expert // batches, tile), lambda n: (0, n, 0))],
        out_specs=pl.BlockSpec((side, packed_rows // batches, tile), lambda n: (0, n, 0)),
        out_shape=jax.ShapeDtypeStruct((side, packed_rows, tile), BF16),
        compiler_params=params("arbitrary"),
        cost_estimate=cost(per_expert * tile * tile, 4 * per_expert * tile * side),
        name="hidden",
    )(swapped.reshape(side, per_expert, tile))
    gathered = exchange(mine.reshape(side * packed_rows, tile), across)
    expert_out = pl.pallas_call(
        functools.partial(down_kernel, batches),
        grid_spec=pltpu.PrefetchScalarGridSpec(
            num_scalar_prefetch=1,
            grid=(1,),
            in_specs=[
                pl.BlockSpec((side, packed_rows, tile), lambda n, me: (0, 0, 0)),
                pl.BlockSpec((1, hidden, features), lambda n, me: (me[0], 0, 0)),
            ]
            + [pl.BlockSpec((features, hidden), lambda n, me: (0, columns // hidden))] * (side - 1),
            out_specs=pl.BlockSpec((side, per_expert, features), lambda n, me: (0, 0, 0)),
        ),
        out_shape=jax.ShapeDtypeStruct((side, per_expert, features), BF16),
        compiler_params=params("arbitrary"),
        cost_estimate=cost(2 * slots * features * hidden, 8 * features * hidden),
        name="down",
    )(me_ref, gathered.reshape(side, packed_rows, tile), w_down, *line_weights)
    returned = exchange(expert_out.reshape(slots, features), along)
    by_source = pl.pallas_call(
        functools.partial(to_sources_kernel, cap, group, sources),
        out_shape=jax.ShapeDtypeStruct((slots, features), BF16),
        compiler_params=params(),
        cost_estimate=cost(2 * slots * features * 320, 4 * slots * features),
        name="to_sources",
    )(returned.reshape(group, per_expert, features))
    weights = pl.pallas_call(
        functools.partial(gate_kernel, cap, experts),
        out_shape=jax.ShapeDtypeStruct((3, rows, slots), BF16),
        compiler_params=params(),
        cost_estimate=cost(8 * rows * experts * slots, 6 * rows * slots),
        name="gate_weights",
    )(routes, gates)
    home = lax.all_to_all(by_source, "outer", split_axis=0, concat_axis=0, tiled=True)
    return pl.pallas_call(
        mix_kernel,
        out_shape=jax.ShapeDtypeStruct((rows, features), BF16),
        compiler_params=params(),
        cost_estimate=cost(6 * rows * slots * features, 2 * slots * features),
        name="mix",
    )(tokens, weights, home)


def solution(mesh):
    in_specs = (
        P("outer", "inner"),
        P("outer", None),
        P("outer", None),
        P("outer", "inner", None),
        P("outer", None, "inner"),
    )
    return jax.shard_map(
        functools.partial(per_device, (mesh.shape["outer"], mesh.shape["inner"])),
        mesh=mesh,
        in_specs=in_specs,
        out_specs=P("outer", "inner"),
        check_vma=False,
    )
```

```python
import functools

import jax
import jax.numpy as jnp
from jax import lax
from jax.experimental import pallas as pl
from jax.experimental.pallas import tpu as pltpu
from jax.sharding import PartitionSpec as P

F32 = jnp.float32
BF16 = jnp.bfloat16
VMEM_LIMIT = 40 * 1024 * 1024


def iota(shape, dim):
    return lax.broadcasted_iota(jnp.int32, shape, dim)


def dot(a, b, contract=((1,), (0,))):
    return lax.dot_general(a, b, (contract, ((), ())), preferred_element_type=F32)


def slot_codes(named):
    rows = named.shape[1]
    earlier = jnp.where(iota((rows, rows), 0) < iota((rows, rows), 1), 1.0, 0.0).astype(BF16)
    rank = dot(named.astype(BF16), earlier)
    return named * (rank + 1.0)


def message_rows(group, shape, dim, fold):
    row = iota(shape, dim)
    each = shape[dim] // group
    position = row // each
    rest = row % each
    return (rest // 2) * group + position, (rest % 2) * fold + 1


def routed(routes_ref, experts):
    top, rows = routes_ref.shape
    expert = iota((experts, rows), 0)
    named = jnp.zeros((experts, rows), F32)
    for k in range(top):
        named = named + jnp.where(routes_ref[k : k + 1, :] == expert, 1.0, 0.0)
    return named


def pack_kernel(group, experts, fold, routes_ref, tokens_ref, packed_ref):
    count = packed_ref.shape[0]
    features = tokens_ref.shape[1]
    code = slot_codes(routed(routes_ref, experts)).astype(BF16)
    expert, first = message_rows(group, (count, 1), 0, fold)
    spread = jnp.where(expert == iota((count, experts), 1), 1.0, 0.0).astype(BF16)
    seen = dot(spread, code) - first.astype(F32)
    tokens = tokens_ref[...]
    for q in range(fold):
        placing = jnp.where(seen == q, 1.0, 0.0).astype(BF16)
        packed_ref[:, q * features : (q + 1) * features] = dot(placing, tokens).astype(BF16)


def gate_kernel(group, experts, fold, routes_ref, gates_ref, weights_ref):
    top, rows = routes_ref.shape
    count = weights_ref.shape[2] // fold
    expert = iota((experts, rows), 0)
    gate = jnp.zeros((experts, rows), F32)
    for k in range(top):
        gate = gate + jnp.where(routes_ref[k : k + 1, :] == expert, gates_ref[k : k + 1, :], 0.0)
    code = slot_codes(routed(routes_ref, experts)).T.astype(BF16)
    gate = gate.T
    expert, first = message_rows(group, (1, count), 1, fold)
    spread = jnp.where(expert == iota((experts, count), 0), 1.0, 0.0).astype(BF16)
    seen = dot(code, spread) - first.astype(F32)
    for part in range(weights_ref.shape[0]):
        piece = gate.astype(BF16)
        gate = gate - piece.astype(F32)
        chosen = dot(piece, spread)
        for q in range(fold):
            weights_ref[part, :, q * count : (q + 1) * count] = jnp.where(
                seen == q, chosen, 0.0
            ).astype(BF16)


def up_kernel(fold, me_ref, arrived_ref, own_ref, *refs):
    others, out_ref, rows_ref = refs[:-2], refs[-2], refs[-1]
    side, _, features = rows_ref.shape
    each = arrived_ref.shape[0] // side
    tile = out_ref.shape[2]

    @pl.when(pl.program_id(0) == 0)
    def _():
        for s in range(side):
            for q in range(fold):
                rows_ref[s, q * each : (q + 1) * each, :] = arrived_ref[
                    s * each : (s + 1) * each, q * features : (q + 1) * features
                ]

    total = dot(rows_ref[me_ref[0]], own_ref[0])
    for k, w_ref in enumerate(others, 1):
        total = total + dot(rows_ref[lax.rem(me_ref[0] + side - k, side)], w_ref[...])
    for n in range(out_ref.shape[0]):
        out_ref[n] = total[:, n * tile : (n + 1) * tile].astype(BF16)


def hidden_kernel(share, parts_ref, out_ref):
    total = parts_ref[0].astype(F32)
    for n in range(1, parts_ref.shape[0]):
        total = total + parts_ref[n].astype(F32)
    width = total.shape[1]
    up = pltpu.roll(total, width - share, 1)
    mixed = (total / (1.0 + jnp.exp(-total)) * up).astype(BF16)
    column = iota((width, 1), 0)
    block = jnp.zeros_like(column)
    for n in range(1, width // (2 * share)):
        block = block + jnp.where(column >= 2 * share * n, 1, 0)
    unit = jnp.where(column - 2 * share * block < share, column - share * block, -width)
    lane = iota((width, width), 1)
    left = jnp.where(unit == lane, 1.0, 0.0).astype(BF16)
    right = jnp.where(unit + width // 2 == lane, 1.0, 0.0).astype(BF16)
    half = total.shape[0] // 2
    hidden = (dot(mixed[:half], left) + dot(mixed[half:], right)).astype(BF16)
    for n in range(out_ref.shape[0]):
        out_ref[n] = hidden


def down_kernel(batches, fold, me_ref, hidden_ref, own_ref, *refs):
    others, out_ref = refs[:-1], refs[-1]
    side, packed, width = hidden_ref.shape
    each = out_ref.shape[0] // side
    features = out_ref.shape[1] // fold
    half = packed // batches
    left = jnp.concatenate([hidden_ref[b, :, : width // 2] for b in range(side)], axis=1)
    right = jnp.concatenate([hidden_ref[b, :, width // 2 :] for b in range(side)], axis=1)
    pieces = []
    for n in range(batches):
        pieces += [left[n * half : (n + 1) * half], right[n * half : (n + 1) * half]]
    hidden = jnp.concatenate(pieces, axis=0)
    for k in range(side):
        w = own_ref[0] if k == 0 else others[k - 1][...]
        made = dot(hidden, w).astype(BF16)
        place = lax.rem(me_ref[0] + side - k, side) if k else me_ref[0]
        for q in range(fold):
            out_ref[
                pl.ds(pl.multiple_of(place * each, each), each), q * features : (q + 1) * features
            ] = made[q * each : (q + 1) * each]


def keep_kernel(*refs):
    sem = refs[-1]
    parts, outs = refs[: len(refs) // 2], refs[len(refs) // 2 : -1]
    copies = [pltpu.make_async_copy(p, o, sem.at[n]) for n, (p, o) in enumerate(zip(parts, outs))]
    for copy in copies:
        copy.start()
    for copy in copies:
        copy.wait()


def mix_kernel(fold, tokens_ref, weights_ref, home_ref, out_ref):
    features = tokens_ref.shape[1]
    home = jnp.concatenate(
        [home_ref[:, q * features : (q + 1) * features] for q in range(fold)], axis=0
    )
    total = tokens_ref[...].astype(F32)
    for part in range(weights_ref.shape[0]):
        total = total + dot(weights_ref[part], home)
    out_ref[...] = total.astype(BF16)


def params(*semantics):
    return pltpu.CompilerParams(
        dimension_semantics=semantics or None, vmem_limit_bytes=VMEM_LIMIT
    )


def cost(flops, nbytes):
    return pl.CostEstimate(flops=flops, bytes_accessed=nbytes, transcendentals=0)


def per_device(mesh_shape, tokens, routes, gates, w_gate_up, w_down):
    rows, features = tokens.shape
    outer, inner = mesh_shape
    group, _, columns = w_gate_up.shape
    hidden = w_down.shape[1]
    experts = group * outer
    cap = 10
    slots = experts * cap
    per_expert = outer * cap
    side = group
    fold = cap // 2
    count = 2 * experts
    across = [[y * side + x for x in range(side)] for y in range(side)]
    along = [[y * side + x for y in range(side)] for x in range(side)]
    column = [[o * inner + n for n in line for o in range(outer)] for line in along]
    me = lax.axis_index("inner") // side
    me_ref = me.astype(jnp.int32).reshape(1)
    in_hbm = functools.partial(pltpu.with_memory_space_constraint, memory_space=pltpu.HBM)

    def exchange(value, axes, groups):
        return lax.all_to_all(
            value, axes, split_axis=0, concat_axis=0, tiled=True, axis_index_groups=groups
        )

    def to_column(messages):
        messages = messages.reshape(experts, 2, fold * features)
        return exchange(messages, ("outer", "inner"), column).reshape(count, fold * features)

    def from_line(weights, k):
        pairs = [(line[n], line[(n + k) % side]) for line in along for n in range(side)]
        share = lax.dynamic_index_in_dim(weights, (me + k) % side, 0, keepdims=False)
        return lax.ppermute(share, "inner", pairs)

    def keep(parts, weight, name):
        return pl.pallas_call(
            keep_kernel,
            in_specs=[pl.BlockSpec(memory_space=pltpu.VMEM)] * len(parts),
            out_specs=[pl.BlockSpec(memory_space=pltpu.HBM)] * len(parts),
            out_shape=[pltpu.HBM(part.shape, BF16) for part in parts],
            scratch_shapes=[pltpu.SemaphoreType.DMA((len(parts),))],
            compiler_params=params(),
            cost_estimate=cost(weight, 4 * len(parts) * parts[0].size),
            name=name,
        )(*parts)

    up_weights = [from_line(w_gate_up, k) for k in range(1, side)]
    up_weights[1:2] = keep(up_weights[1:2], 20000000000, "keep_up")
    up_weights = [in_hbm(part) for part in up_weights]
    down_weights = keep([from_line(w_down, k) for k in range(1, side)], 20000000000, "keep_down")
    routes, gates = routes.T, gates.T

    packed = pl.pallas_call(
        functools.partial(pack_kernel, group, experts, fold),
        out_shape=jax.ShapeDtypeStruct((count, fold * features), BF16),
        compiler_params=params(),
        cost_estimate=cost(4 * slots * rows * features, 2 * slots * features),
        name="pack",
    )(routes, tokens)
    arrived = to_column(packed)

    tile = columns // side
    partial_value = pl.pallas_call(
        functools.partial(up_kernel, fold),
        grid_spec=pltpu.PrefetchScalarGridSpec(
            num_scalar_prefetch=1,
            grid=(side // 2,),
            in_specs=[
                pl.BlockSpec((count, fold * features), lambda c, me: (0, 0)),
                pl.BlockSpec((1, features, 2 * tile), lambda c, me: (me[0], 0, c)),
            ]
            + [pl.BlockSpec((features, 2 * tile), lambda c, me: (0, c))] * (side - 1),
            out_specs=pl.BlockSpec((2, per_expert, tile), lambda c, me: (c, 0, 0)),
            scratch_shapes=[pltpu.VMEM((side, per_expert, features), BF16)],
        ),
        out_shape=jax.ShapeDtypeStruct((side, per_expert, tile), BF16),
        compiler_params=params("arbitrary"),
        cost_estimate=cost(2 * slots * features * columns, 8 * features * columns),
        name="gate_up",
    )(me_ref, arrived, in_hbm(w_gate_up), *up_weights)
    swapped = exchange(partial_value.reshape(side * per_expert, tile), "inner", across)
    swapped, *down_weights = lax.optimization_barrier((swapped, *down_weights))
    batches = 2
    packed_rows = per_expert // 2
    mine = pl.pallas_call(
        functools.partial(hidden_kernel, hidden // inner),
        grid=(batches,),
        in_specs=[pl.BlockSpec((side, per_expert // batches, tile), lambda n: (0, n, 0))],
        out_specs=pl.BlockSpec((side, packed_rows // batches, tile), lambda n: (0, n, 0)),
        out_shape=jax.ShapeDtypeStruct((side, packed_rows, tile), BF16),
        compiler_params=params("arbitrary"),
        cost_estimate=cost(per_expert * tile * tile, 4 * per_expert * tile * side),
        name="hidden",
    )(swapped.reshape(side, per_expert, tile))
    gathered = exchange(mine.reshape(side * packed_rows, tile), "inner", across)
    expert_out = pl.pallas_call(
        functools.partial(down_kernel, batches, fold),
        grid_spec=pltpu.PrefetchScalarGridSpec(
            num_scalar_prefetch=1,
            grid=(1,),
            in_specs=[
                pl.BlockSpec((side, packed_rows, tile), lambda n, me: (0, 0, 0)),
                pl.BlockSpec((1, hidden, features), lambda n, me: (me[0], 0, 0)),
            ]
            + [pl.BlockSpec((hidden, features), lambda n, me: (0, 0))] * (side - 1),
            out_specs=pl.BlockSpec((count, fold * features), lambda n, me: (0, 0)),
        ),
        out_shape=jax.ShapeDtypeStruct((count, fold * features), BF16),
        compiler_params=params("arbitrary"),
        cost_estimate=cost(2 * slots * features * hidden, 8 * features * hidden),
        name="down",
    )(me_ref, gathered.reshape(side, packed_rows, tile), in_hbm(w_down), *map(in_hbm, down_weights))
    weights = pl.pallas_call(
        functools.partial(gate_kernel, group, experts, fold),
        out_shape=jax.ShapeDtypeStruct((3, rows, slots), BF16),
        compiler_params=params(),
        cost_estimate=cost(2 * rows * experts * slots, 6 * rows * slots),
        name="gate_weights",
    )(routes, gates)
    home = to_column(expert_out)
    return pl.pallas_call(
        functools.partial(mix_kernel, fold),
        out_shape=jax.ShapeDtypeStruct((rows, features), BF16),
        compiler_params=params(),
        cost_estimate=cost(6 * rows * slots * features, 2 * slots * features),
        name="mix",
    )(tokens, weights, home)


def solution(mesh):
    in_specs = (
        P("outer", "inner"),
        P("outer", None),
        P("outer", None),
        P("outer", "inner", None),
        P("outer", None, "inner"),
    )
    return jax.shard_map(
        functools.partial(per_device, (mesh.shape["outer"], mesh.shape["inner"])),
        mesh=mesh,
        in_specs=in_specs,
        out_specs=P("outer", "inner"),
        check_vma=False,
    )
```

```python
import functools

import jax
import jax.numpy as jnp
from jax import lax
from jax.experimental import pallas as pl
from jax.experimental.pallas import tpu as pltpu
from jax.sharding import PartitionSpec as P

F32 = jnp.float32
BF16 = jnp.bfloat16
VMEM_LIMIT = 40 * 1024 * 1024


def iota(shape, dim):
    return lax.broadcasted_iota(jnp.int32, shape, dim)


def dot(a, b, contract=((1,), (0,))):
    return lax.dot_general(a, b, (contract, ((), ())), preferred_element_type=F32)


def slot_codes(named):
    rows = named.shape[1]
    earlier = jnp.where(iota((rows, rows), 0) < iota((rows, rows), 1), 1.0, 0.0).astype(BF16)
    rank = dot(named.astype(BF16), earlier)
    return named * (rank + 1.0)


def message_rows(group, shape, dim, fold):
    row = iota(shape, dim)
    each = shape[dim] // group
    position = row // each
    rest = row % each
    return (rest // 2) * group + position, (rest % 2) * fold + 1


def routed(routes_ref, experts):
    top, rows = routes_ref.shape
    expert = iota((experts, rows), 0)
    named = jnp.zeros((experts, rows), F32)
    for k in range(top):
        named = named + jnp.where(routes_ref[k : k + 1, :] == expert, 1.0, 0.0)
    return named


def pack_kernel(group, experts, fold, routes_in, tokens_in, packed_ref, routes_ref, tokens_ref, sem):
    loads = [
        pltpu.make_async_copy(routes_in, routes_ref, sem.at[0]),
        pltpu.make_async_copy(tokens_in, tokens_ref, sem.at[1]),
    ]
    for load in loads:
        load.start()
    for load in loads:
        load.wait()
    count = packed_ref.shape[0]
    features = tokens_ref.shape[1]
    code = slot_codes(routed(routes_ref, experts)).astype(BF16)
    expert, first = message_rows(group, (count, 1), 0, fold)
    spread = jnp.where(expert == iota((count, experts), 1), 1.0, 0.0).astype(BF16)
    seen = dot(spread, code) - first.astype(F32)
    tokens = tokens_ref[...]
    for q in range(fold):
        placing = jnp.where(seen == q, 1.0, 0.0).astype(BF16)
        packed_ref[:, q * features : (q + 1) * features] = dot(placing, tokens).astype(BF16)


def gate_kernel(group, experts, fold, routes_ref, gates_ref, weights_ref):
    top, rows = routes_ref.shape
    count = weights_ref.shape[2] // fold
    expert = iota((experts, rows), 0)
    gate = jnp.zeros((experts, rows), F32)
    for k in range(top):
        gate = gate + jnp.where(routes_ref[k : k + 1, :] == expert, gates_ref[k : k + 1, :], 0.0)
    code = slot_codes(routed(routes_ref, experts)).T.astype(BF16)
    gate = gate.T
    expert, first = message_rows(group, (1, count), 1, fold)
    spread = jnp.where(expert == iota((experts, count), 0), 1.0, 0.0).astype(BF16)
    seen = dot(code, spread) - first.astype(F32)
    for part in range(weights_ref.shape[0]):
        piece = gate.astype(BF16)
        gate = gate - piece.astype(F32)
        chosen = dot(piece, spread)
        for q in range(fold):
            weights_ref[part, :, q * count : (q + 1) * count] = jnp.where(
                seen == q, chosen, 0.0
            ).astype(BF16)


def up_kernel(fold, me_ref, arrived_ref, own_ref, *refs):
    others, out_ref, rows_ref = refs[:-2], refs[-2], refs[-1]
    side, _, features = rows_ref.shape
    each = arrived_ref.shape[0] // side
    tile = out_ref.shape[2]

    @pl.when(pl.program_id(0) == 0)
    def _():
        for s in range(side):
            for q in range(fold):
                rows_ref[s, q * each : (q + 1) * each, :] = arrived_ref[
                    s * each : (s + 1) * each, q * features : (q + 1) * features
                ]

    total = dot(rows_ref[me_ref[0]], own_ref[0])
    for k, w_ref in enumerate(others, 1):
        total = total + dot(rows_ref[lax.rem(me_ref[0] + side - k, side)], w_ref[...])
    for n in range(out_ref.shape[0]):
        out_ref[n] = total[:, n * tile : (n + 1) * tile].astype(BF16)


def hidden_kernel(share, parts_ref, out_ref):
    total = parts_ref[0].astype(F32)
    for n in range(1, parts_ref.shape[0]):
        total = total + parts_ref[n].astype(F32)
    width = total.shape[1]
    up = pltpu.roll(total, width - share, 1)
    mixed = (total / (1.0 + jnp.exp(-total)) * up).astype(BF16)
    column = iota((width, 1), 0)
    block = jnp.zeros_like(column)
    for n in range(1, width // (2 * share)):
        block = block + jnp.where(column >= 2 * share * n, 1, 0)
    unit = jnp.where(column - 2 * share * block < share, column - share * block, -width)
    lane = iota((width, width), 1)
    left = jnp.where(unit == lane, 1.0, 0.0).astype(BF16)
    right = jnp.where(unit + width // 2 == lane, 1.0, 0.0).astype(BF16)
    half = total.shape[0] // 2
    hidden = (dot(mixed[:half], left) + dot(mixed[half:], right)).astype(BF16)
    for n in range(out_ref.shape[0]):
        out_ref[n] = hidden


def down_kernel(batches, fold, me_ref, hidden_ref, own_ref, *refs):
    others, out_ref = refs[:-1], refs[-1]
    side, packed, width = hidden_ref.shape
    each = out_ref.shape[0] // side
    features = out_ref.shape[1] // fold
    half = packed // batches
    left = jnp.concatenate([hidden_ref[b, :, : width // 2] for b in range(side)], axis=1)
    right = jnp.concatenate([hidden_ref[b, :, width // 2 :] for b in range(side)], axis=1)
    pieces = []
    for n in range(batches):
        pieces += [left[n * half : (n + 1) * half], right[n * half : (n + 1) * half]]
    hidden = jnp.concatenate(pieces, axis=0)
    for k in range(side):
        w = own_ref[0] if k == 0 else others[k - 1][...]
        made = dot(hidden, w).astype(BF16)
        place = lax.rem(me_ref[0] + side - k, side) if k else me_ref[0]
        for q in range(fold):
            out_ref[
                pl.ds(pl.multiple_of(place * each, each), each), q * features : (q + 1) * features
            ] = made[q * each : (q + 1) * each]


def take_kernel(me_ref, weights_ref, out_ref):
    out_ref[...] = weights_ref[0]


def stay_kernel(in_ref, out_ref):
    pass


def keep_kernel(*refs):
    sem = refs[-1]
    parts, outs = refs[: len(refs) // 2], refs[len(refs) // 2 : -1]
    copies = [pltpu.make_async_copy(p, o, sem.at[n]) for n, (p, o) in enumerate(zip(parts, outs))]
    for copy in copies:
        copy.start()
    for copy in copies:
        copy.wait()


def mix_kernel(fold, tokens_ref, weights_ref, home_ref, out_ref):
    features = tokens_ref.shape[1]
    home = jnp.concatenate(
        [home_ref[:, q * features : (q + 1) * features] for q in range(fold)], axis=0
    )
    total = tokens_ref[...].astype(F32)
    for part in range(weights_ref.shape[0]):
        total = total + dot(weights_ref[part], home)
    out_ref[...] = total.astype(BF16)


def params(*semantics):
    return pltpu.CompilerParams(
        dimension_semantics=semantics or None, vmem_limit_bytes=VMEM_LIMIT
    )


def cost(flops, nbytes):
    return pl.CostEstimate(flops=flops, bytes_accessed=nbytes, transcendentals=0)


def per_device(mesh_shape, tokens, routes, gates, w_gate_up, w_down):
    rows, features = tokens.shape
    outer, inner = mesh_shape
    group, _, columns = w_gate_up.shape
    hidden = w_down.shape[1]
    experts = group * outer
    cap = 10
    slots = experts * cap
    per_expert = outer * cap
    side = group
    fold = cap // 2
    count = 2 * experts
    across = [[y * side + x for x in range(side)] for y in range(side)]
    along = [[y * side + x for y in range(side)] for x in range(side)]
    column = [[o * inner + n for n in line for o in range(outer)] for line in along]
    me = lax.axis_index("inner") // side
    me_ref = me.astype(jnp.int32).reshape(1)
    hbm = pl.BlockSpec(memory_space=pltpu.HBM)
    in_hbm = functools.partial(pltpu.with_memory_space_constraint, memory_space=pltpu.HBM)

    def exchange(value, axes, groups):
        return lax.all_to_all(
            value, axes, split_axis=0, concat_axis=0, tiled=True, axis_index_groups=groups
        )

    def to_column(messages):
        messages = messages.reshape(experts, 2, fold * features)
        got = exchange(messages, ("outer", "inner"), column)
        got = pl.pallas_call(
            stay_kernel,
            in_specs=[pl.BlockSpec(memory_space=pltpu.VMEM)],
            out_specs=pl.BlockSpec(memory_space=pltpu.VMEM),
            out_shape=pltpu.VMEM(got.shape, got.dtype),
            input_output_aliases={0: 0},
            compiler_params=params(),
            cost_estimate=cost(1, 1),
            name="arrived",
        )(pltpu.with_memory_space_constraint(got, pltpu.VMEM))
        return got.reshape(count, fold * features)

    def take(weights, k):
        _, *share = weights.shape
        return pl.pallas_call(
            take_kernel,
            grid_spec=pltpu.PrefetchScalarGridSpec(
                num_scalar_prefetch=1,
                grid=(1,),
                in_specs=[pl.BlockSpec((1, *share), lambda n, me: (lax.rem(me[0] + k, side), 0, 0))],
                out_specs=pl.BlockSpec(share, lambda n, me: (0, 0)),
            ),
            out_shape=pltpu.HBM(share, BF16),
            compiler_params=params("arbitrary"),
            cost_estimate=cost(1, 4 * share[0] * share[1]),
            name="take",
        )(me_ref, in_hbm(weights))

    def from_line(weights, k, taken=None):
        pairs = [(line[n], line[(n + k) % side]) for line in along for n in range(side)]
        if taken is None:
            taken = lax.dynamic_index_in_dim(weights, (me + k) % side, 0, keepdims=False)
        return lax.ppermute(taken, "inner", pairs)

    def keep(parts, weight, name):
        return pl.pallas_call(
            keep_kernel,
            in_specs=[pl.BlockSpec(memory_space=pltpu.VMEM)] * len(parts),
            out_specs=[pl.BlockSpec(memory_space=pltpu.HBM)] * len(parts),
            out_shape=[pltpu.HBM(part.shape, BF16) for part in parts],
            scratch_shapes=[pltpu.SemaphoreType.DMA((len(parts),))],
            compiler_params=params(),
            cost_estimate=cost(weight, 4 * len(parts) * parts[0].size),
            name=name,
        )(*parts)

    (far,) = keep([from_line(w_gate_up, 2)], 20000000000, "keep_up")
    routes, gates = routes.T, gates.T

    packed = pl.pallas_call(
        functools.partial(pack_kernel, group, experts, fold),
        in_specs=[hbm, hbm],
        out_specs=pl.BlockSpec(memory_space=pltpu.VMEM),
        scratch_shapes=[
            pltpu.VMEM(routes.shape, routes.dtype),
            pltpu.VMEM(tokens.shape, tokens.dtype),
            pltpu.SemaphoreType.DMA((2,)),
        ],
        out_shape=jax.ShapeDtypeStruct((count, fold * features), BF16),
        compiler_params=params(),
        cost_estimate=cost(4 * slots * rows * features, 2 * slots * features),
        name="pack",
    )(in_hbm(routes), in_hbm(tokens))
    packed, up_late, down_late = lax.optimization_barrier((packed, w_gate_up, w_down))
    arrived = to_column(packed)
    near = [from_line(up_late, k, take(up_late, k)) for k in (1, 3)]
    up_weights = [near[0], far, near[1]]
    up_weights = [in_hbm(part) for part in up_weights]
    down_weights = keep([from_line(down_late, k) for k in range(1, side)], 20000000000, "keep_down")

    tile = columns // side
    partial_value = pl.pallas_call(
        functools.partial(up_kernel, fold),
        grid_spec=pltpu.PrefetchScalarGridSpec(
            num_scalar_prefetch=1,
            grid=(side // 2,),
            in_specs=[
                pl.BlockSpec((count, fold * features), lambda c, me: (0, 0)),
                pl.BlockSpec((1, features, 2 * tile), lambda c, me: (me[0], 0, c)),
            ]
            + [pl.BlockSpec((features, 2 * tile), lambda c, me: (0, c))] * (side - 1),
            out_specs=pl.BlockSpec((2, per_expert, tile), lambda c, me: (c, 0, 0)),
            scratch_shapes=[pltpu.VMEM((side, per_expert, features), BF16)],
        ),
        out_shape=jax.ShapeDtypeStruct((side, per_expert, tile), BF16),
        compiler_params=params("arbitrary"),
        cost_estimate=cost(2 * slots * features * columns, 8 * features * columns),
        name="gate_up",
    )(me_ref, arrived, in_hbm(w_gate_up), *up_weights)
    swapped = exchange(partial_value.reshape(side * per_expert, tile), "inner", across)
    swapped, *down_weights = lax.optimization_barrier((swapped, *down_weights))
    batches = 2
    packed_rows = per_expert // 2
    mine = pl.pallas_call(
        functools.partial(hidden_kernel, hidden // inner),
        grid=(batches,),
        in_specs=[pl.BlockSpec((side, per_expert // batches, tile), lambda n: (0, n, 0))],
        out_specs=pl.BlockSpec((side, packed_rows // batches, tile), lambda n: (0, n, 0)),
        out_shape=jax.ShapeDtypeStruct((side, packed_rows, tile), BF16),
        compiler_params=params("arbitrary"),
        cost_estimate=cost(per_expert * tile * tile, 4 * per_expert * tile * side),
        name="hidden",
    )(swapped.reshape(side, per_expert, tile))
    gathered = exchange(mine.reshape(side * packed_rows, tile), "inner", across)
    expert_out = pl.pallas_call(
        functools.partial(down_kernel, batches, fold),
        grid_spec=pltpu.PrefetchScalarGridSpec(
            num_scalar_prefetch=1,
            grid=(1,),
            in_specs=[
                pl.BlockSpec((side, packed_rows, tile), lambda n, me: (0, 0, 0)),
                pl.BlockSpec((1, hidden, features), lambda n, me: (me[0], 0, 0)),
            ]
            + [pl.BlockSpec((hidden, features), lambda n, me: (0, 0))] * (side - 1),
            out_specs=pl.BlockSpec((count, fold * features), lambda n, me: (0, 0)),
        ),
        out_shape=jax.ShapeDtypeStruct((count, fold * features), BF16),
        compiler_params=params("arbitrary"),
        cost_estimate=cost(2 * slots * features * hidden, 8 * features * hidden),
        name="down",
    )(me_ref, gathered.reshape(side, packed_rows, tile), in_hbm(w_down), *map(in_hbm, down_weights))
    weights = pl.pallas_call(
        functools.partial(gate_kernel, group, experts, fold),
        out_shape=jax.ShapeDtypeStruct((3, rows, slots), BF16),
        compiler_params=params(),
        cost_estimate=cost(2 * rows * experts * slots, 6 * rows * slots),
        name="gate_weights",
    )(routes, gates)
    home = to_column(expert_out)
    return pl.pallas_call(
        functools.partial(mix_kernel, fold),
        out_shape=jax.ShapeDtypeStruct((rows, features), BF16),
        compiler_params=params(),
        cost_estimate=cost(6 * rows * slots * features, 2 * slots * features),
        name="mix",
    )(tokens, weights, home)


def solution(mesh):
    in_specs = (
        P("outer", "inner"),
        P("outer", None),
        P("outer", None),
        P("outer", "inner", None),
        P("outer", None, "inner"),
    )
    return jax.shard_map(
        functools.partial(per_device, (mesh.shape["outer"], mesh.shape["inner"])),
        mesh=mesh,
        in_specs=in_specs,
        out_specs=P("outer", "inner"),
        check_vma=False,
    )
```

```python
import functools

import jax
import jax.numpy as jnp
from jax import lax
from jax.experimental import pallas as pl
from jax.experimental.pallas import tpu as pltpu
from jax.sharding import PartitionSpec as P

F32 = jnp.float32
BF16 = jnp.bfloat16
VMEM_LIMIT = 40 * 1024 * 1024


def iota(shape, dim):
    return lax.broadcasted_iota(jnp.int32, shape, dim)


def dot(a, b, contract=((1,), (0,))):
    return lax.dot_general(a, b, (contract, ((), ())), preferred_element_type=F32)


def slot_codes(named):
    rows = named.shape[1]
    earlier = jnp.where(iota((rows, rows), 0) < iota((rows, rows), 1), 1.0, 0.0).astype(BF16)
    rank = dot(named.astype(BF16), earlier)
    return named * (rank + 1.0)


def message_rows(group, shape, dim, fold):
    row = iota(shape, dim)
    each = shape[dim] // group
    position = row // each
    rest = row % each
    return (rest // 2) * group + position, (rest % 2) * fold + 1


def routed(routes_ref, experts):
    top, rows = routes_ref.shape
    expert = iota((experts, rows), 0)
    named = jnp.zeros((experts, rows), F32)
    for k in range(top):
        named = named + jnp.where(routes_ref[k : k + 1, :] == expert, 1.0, 0.0)
    return named


def pack_kernel(group, experts, fold, routes_in, tokens_in, packed_ref, routes_ref, tokens_ref, sem):
    loads = [
        pltpu.make_async_copy(routes_in, routes_ref, sem.at[0]),
        pltpu.make_async_copy(tokens_in, tokens_ref, sem.at[1]),
    ]
    for load in loads:
        load.start()
    for load in loads:
        load.wait()
    count = packed_ref.shape[0]
    features = tokens_ref.shape[1]
    code = slot_codes(routed(routes_ref, experts)).astype(BF16)
    expert, first = message_rows(group, (count, 1), 0, fold)
    spread = jnp.where(expert == iota((count, experts), 1), 1.0, 0.0).astype(BF16)
    seen = dot(spread, code) - first.astype(F32)
    tokens = tokens_ref[...]
    for q in range(fold):
        placing = jnp.where(seen == q, 1.0, 0.0).astype(BF16)
        packed_ref[:, q * features : (q + 1) * features] = dot(placing, tokens).astype(BF16)


def gate_kernel(group, experts, fold, routes_ref, gates_ref, weights_ref):
    top, rows = routes_ref.shape
    count = weights_ref.shape[2] // fold
    expert = iota((experts, rows), 0)
    gate = jnp.zeros((experts, rows), F32)
    for k in range(top):
        gate = gate + jnp.where(routes_ref[k : k + 1, :] == expert, gates_ref[k : k + 1, :], 0.0)
    code = slot_codes(routed(routes_ref, experts)).T.astype(BF16)
    gate = gate.T
    expert, first = message_rows(group, (1, count), 1, fold)
    spread = jnp.where(expert == iota((experts, count), 0), 1.0, 0.0).astype(BF16)
    seen = dot(code, spread) - first.astype(F32)
    for part in range(weights_ref.shape[0]):
        piece = gate.astype(BF16)
        gate = gate - piece.astype(F32)
        chosen = dot(piece, spread)
        for q in range(fold):
            weights_ref[part, :, q * count : (q + 1) * count] = jnp.where(
                seen == q, chosen, 0.0
            ).astype(BF16)


def up_kernel(fold, me_ref, arrived_ref, own_ref, *refs):
    others, out_ref, rows_ref = refs[:-2], refs[-2], refs[-1]
    side, _, features = rows_ref.shape
    each = arrived_ref.shape[0] // side
    tile = out_ref.shape[2]

    @pl.when(pl.program_id(0) == 0)
    def _():
        for s in range(side):
            for q in range(fold):
                rows_ref[s, q * each : (q + 1) * each, :] = arrived_ref[
                    s * each : (s + 1) * each, q * features : (q + 1) * features
                ]

    total = dot(rows_ref[me_ref[0]], own_ref[0])
    for k, w_ref in enumerate(others, 1):
        total = total + dot(rows_ref[lax.rem(me_ref[0] + side - k, side)], w_ref[...])
    for n in range(out_ref.shape[0]):
        out_ref[n] = total[:, n * tile : (n + 1) * tile].astype(BF16)


def hidden_kernel(share, parts_ref, out_ref):
    total = parts_ref[0].astype(F32)
    for n in range(1, parts_ref.shape[0]):
        total = total + parts_ref[n].astype(F32)
    width = total.shape[1]
    up = pltpu.roll(total, width - share, 1)
    mixed = (total / (1.0 + jnp.exp(-total)) * up).astype(BF16)
    column = iota((width, 1), 0)
    block = jnp.zeros_like(column)
    for n in range(1, width // (2 * share)):
        block = block + jnp.where(column >= 2 * share * n, 1, 0)
    unit = jnp.where(column - 2 * share * block < share, column - share * block, -width)
    lane = iota((width, width), 1)
    left = jnp.where(unit == lane, 1.0, 0.0).astype(BF16)
    right = jnp.where(unit + width // 2 == lane, 1.0, 0.0).astype(BF16)
    half = total.shape[0] // 2
    hidden = (dot(mixed[:half], left) + dot(mixed[half:], right)).astype(BF16)
    for n in range(out_ref.shape[0]):
        out_ref[n] = hidden


def down_kernel(batches, fold, me_ref, hidden_ref, own_ref, *refs):
    others, out_ref = refs[:-1], refs[-1]
    side, packed, width = hidden_ref.shape
    each = out_ref.shape[0] // side
    features = out_ref.shape[1] // fold
    half = packed // batches
    left = jnp.concatenate([hidden_ref[b, :, : width // 2] for b in range(side)], axis=1)
    right = jnp.concatenate([hidden_ref[b, :, width // 2 :] for b in range(side)], axis=1)
    pieces = []
    for n in range(batches):
        pieces += [left[n * half : (n + 1) * half], right[n * half : (n + 1) * half]]
    hidden = jnp.concatenate(pieces, axis=0)
    for k in range(side):
        w = own_ref[0] if k == 0 else others[k - 1][...]
        made = dot(hidden, w).astype(BF16)
        place = lax.rem(me_ref[0] + side - k, side) if k else me_ref[0]
        for q in range(fold):
            out_ref[
                pl.ds(pl.multiple_of(place * each, each), each), q * features : (q + 1) * features
            ] = made[q * each : (q + 1) * each]


def take_kernel(me_ref, weights_ref, out_ref):
    out_ref[...] = weights_ref[0]


def keep_kernel(*refs):
    sem = refs[-1]
    parts, outs = refs[: len(refs) // 2], refs[len(refs) // 2 : -1]
    copies = [pltpu.make_async_copy(p, o, sem.at[n]) for n, (p, o) in enumerate(zip(parts, outs))]
    for copy in copies:
        copy.start()
    for copy in copies:
        copy.wait()


def mix_kernel(fold, tokens_ref, weights_ref, home_ref, out_ref):
    features = tokens_ref.shape[1]
    home = jnp.concatenate(
        [home_ref[:, q * features : (q + 1) * features] for q in range(fold)], axis=0
    )
    total = tokens_ref[...].astype(F32)
    for part in range(weights_ref.shape[0]):
        total = total + dot(weights_ref[part], home)
    out_ref[...] = total.astype(BF16)


def params(*semantics):
    return pltpu.CompilerParams(
        dimension_semantics=semantics or None, vmem_limit_bytes=VMEM_LIMIT
    )


def cost(flops, nbytes):
    return pl.CostEstimate(flops=flops, bytes_accessed=nbytes, transcendentals=0)


def per_device(mesh_shape, tokens, routes, gates, w_gate_up, w_down):
    rows, features = tokens.shape
    outer, inner = mesh_shape
    group, _, columns = w_gate_up.shape
    hidden = w_down.shape[1]
    experts = group * outer
    cap = 10
    slots = experts * cap
    per_expert = outer * cap
    side = group
    fold = cap // 2
    count = 2 * experts
    across = [[y * side + x for x in range(side)] for y in range(side)]
    along = [[y * side + x for y in range(side)] for x in range(side)]
    column = [[o * inner + n for n in line for o in range(outer)] for line in along]
    me = lax.axis_index("inner") // side
    me_ref = me.astype(jnp.int32).reshape(1)
    hbm = pl.BlockSpec(memory_space=pltpu.HBM)
    in_hbm = functools.partial(pltpu.with_memory_space_constraint, memory_space=pltpu.HBM)

    def exchange(value, axes, groups):
        return lax.all_to_all(
            value, axes, split_axis=0, concat_axis=0, tiled=True, axis_index_groups=groups
        )

    def to_column(messages):
        messages = messages.reshape(experts, 2, fold * features)
        got = exchange(messages, ("outer", "inner"), column)
        return got.reshape(count, fold * features)

    def take(weights, k):
        _, *share = weights.shape
        return pl.pallas_call(
            take_kernel,
            grid_spec=pltpu.PrefetchScalarGridSpec(
                num_scalar_prefetch=1,
                grid=(1,),
                in_specs=[pl.BlockSpec((1, *share), lambda n, me: (lax.rem(me[0] + k, side), 0, 0))],
                out_specs=pl.BlockSpec(share, lambda n, me: (0, 0)),
            ),
            out_shape=pltpu.HBM(share, BF16),
            compiler_params=params("arbitrary"),
            cost_estimate=cost(1, 4 * share[0] * share[1]),
            name="take",
        )(me_ref, in_hbm(weights))

    def from_line(weights, k, taken=None):
        pairs = [(line[n], line[(n + k) % side]) for line in along for n in range(side)]
        if taken is None:
            taken = lax.dynamic_index_in_dim(weights, (me + k) % side, 0, keepdims=False)
        return lax.ppermute(taken, "inner", pairs)

    def keep(parts, weight, name):
        return pl.pallas_call(
            keep_kernel,
            in_specs=[pl.BlockSpec(memory_space=pltpu.VMEM)] * len(parts),
            out_specs=[pl.BlockSpec(memory_space=pltpu.HBM)] * len(parts),
            out_shape=[pltpu.HBM(part.shape, BF16) for part in parts],
            scratch_shapes=[pltpu.SemaphoreType.DMA((len(parts),))],
            compiler_params=params(),
            cost_estimate=cost(weight, 4 * len(parts) * parts[0].size),
            name=name,
        )(*parts)

    (far,) = keep([from_line(w_gate_up, 2)], 20000000000, "keep_up")
    routes, gates = routes.T, gates.T

    packed = pl.pallas_call(
        functools.partial(pack_kernel, group, experts, fold),
        in_specs=[hbm, hbm],
        out_specs=pl.BlockSpec(memory_space=pltpu.VMEM),
        scratch_shapes=[
            pltpu.VMEM(routes.shape, routes.dtype),
            pltpu.VMEM(tokens.shape, tokens.dtype),
            pltpu.SemaphoreType.DMA((2,)),
        ],
        out_shape=jax.ShapeDtypeStruct((count, fold * features), BF16),
        compiler_params=params(),
        cost_estimate=cost(4 * slots * rows * features, 2 * slots * features),
        name="pack",
    )(in_hbm(routes), in_hbm(tokens))
    packed, up_late, down_late = lax.optimization_barrier((packed, w_gate_up, w_down))
    arrived = to_column(packed)
    near = [from_line(up_late, k, take(up_late, k)) for k in (1, 3)]
    up_weights = [near[0], far, near[1]]
    up_weights = [in_hbm(part) for part in up_weights]
    down_weights = keep([from_line(down_late, k) for k in range(1, side)], 20000000000, "keep_down")

    tile = columns // side
    partial_value = pl.pallas_call(
        functools.partial(up_kernel, fold),
        grid_spec=pltpu.PrefetchScalarGridSpec(
            num_scalar_prefetch=1,
            grid=(side // 2,),
            in_specs=[
                pl.BlockSpec((count, fold * features), lambda c, me: (0, 0)),
                pl.BlockSpec((1, features, 2 * tile), lambda c, me: (me[0], 0, c)),
            ]
            + [pl.BlockSpec((features, 2 * tile), lambda c, me: (0, c))] * (side - 1),
            out_specs=pl.BlockSpec((2, per_expert, tile), lambda c, me: (c, 0, 0)),
            scratch_shapes=[pltpu.VMEM((side, per_expert, features), BF16)],
        ),
        out_shape=jax.ShapeDtypeStruct((side, per_expert, tile), BF16),
        compiler_params=params("arbitrary"),
        cost_estimate=cost(2 * slots * features * columns, 8 * features * columns),
        name="gate_up",
    )(me_ref, arrived, in_hbm(w_gate_up), *up_weights)
    swapped = exchange(partial_value.reshape(side * per_expert, tile), "inner", across)
    swapped, *down_weights = lax.optimization_barrier((swapped, *down_weights))
    batches = 2
    packed_rows = per_expert // 2
    mine = pl.pallas_call(
        functools.partial(hidden_kernel, hidden // inner),
        grid=(batches,),
        in_specs=[pl.BlockSpec((side, per_expert // batches, tile), lambda n: (0, n, 0))],
        out_specs=pl.BlockSpec((side, packed_rows // batches, tile), lambda n: (0, n, 0)),
        out_shape=jax.ShapeDtypeStruct((side, packed_rows, tile), BF16),
        compiler_params=params("arbitrary"),
        cost_estimate=cost(per_expert * tile * tile, 4 * per_expert * tile * side),
        name="hidden",
    )(swapped.reshape(side, per_expert, tile))
    gathered = exchange(mine.reshape(side * packed_rows, tile), "inner", across)
    expert_out = pl.pallas_call(
        functools.partial(down_kernel, batches, fold),
        grid_spec=pltpu.PrefetchScalarGridSpec(
            num_scalar_prefetch=1,
            grid=(1,),
            in_specs=[
                pl.BlockSpec((side, packed_rows, tile), lambda n, me: (0, 0, 0)),
                pl.BlockSpec((1, hidden, features), lambda n, me: (me[0], 0, 0)),
            ]
            + [pl.BlockSpec((hidden, features), lambda n, me: (0, 0))] * (side - 1),
            out_specs=pl.BlockSpec((count, fold * features), lambda n, me: (0, 0)),
        ),
        out_shape=jax.ShapeDtypeStruct((count, fold * features), BF16),
        compiler_params=params("arbitrary"),
        cost_estimate=cost(2 * slots * features * hidden, 8 * features * hidden),
        name="down",
    )(me_ref, gathered.reshape(side, packed_rows, tile), in_hbm(w_down), *map(in_hbm, down_weights))
    weights = pl.pallas_call(
        functools.partial(gate_kernel, group, experts, fold),
        out_shape=jax.ShapeDtypeStruct((3, rows, slots), BF16),
        compiler_params=params(),
        cost_estimate=cost(2 * rows * experts * slots, 6 * rows * slots),
        name="gate_weights",
    )(routes, gates)
    home = to_column(expert_out)
    return pl.pallas_call(
        functools.partial(mix_kernel, fold),
        out_shape=jax.ShapeDtypeStruct((rows, features), BF16),
        compiler_params=params(),
        cost_estimate=cost(6 * rows * slots * features, 2 * slots * features),
        name="mix",
    )(tokens, weights, home)


def solution(mesh):
    in_specs = (
        P("outer", "inner"),
        P("outer", None),
        P("outer", None),
        P("outer", "inner", None),
        P("outer", None, "inner"),
    )
    return jax.shard_map(
        functools.partial(per_device, (mesh.shape["outer"], mesh.shape["inner"])),
        mesh=mesh,
        in_specs=in_specs,
        out_specs=P("outer", "inner"),
        check_vma=False,
    )
```

```python
import functools

import jax
import jax.numpy as jnp
from jax import lax
from jax.experimental import pallas as pl
from jax.experimental.pallas import tpu as pltpu
from jax.sharding import PartitionSpec as P

F32 = jnp.float32
BF16 = jnp.bfloat16
VMEM_LIMIT = 40 * 1024 * 1024


def iota(shape, dim):
    return lax.broadcasted_iota(jnp.int32, shape, dim)


def dot(a, b, contract=((1,), (0,))):
    return lax.dot_general(a, b, (contract, ((), ())), preferred_element_type=F32)


def slot_codes(named):
    rows = named.shape[1]
    earlier = jnp.where(iota((rows, rows), 0) < iota((rows, rows), 1), 1.0, 0.0).astype(BF16)
    rank = dot(named.astype(BF16), earlier)
    return named * (rank + 1.0)


def message_rows(group, shape, dim, fold):
    row = iota(shape, dim)
    each = shape[dim] // group
    position = row // each
    rest = row % each
    return (rest // 2) * group + position, (rest % 2) * fold + 1


def routed(routes_ref, experts):
    top, rows = routes_ref.shape
    expert = iota((experts, rows), 0)
    named = jnp.zeros((experts, rows), F32)
    for k in range(top):
        named = named + jnp.where(routes_ref[k : k + 1, :] == expert, 1.0, 0.0)
    return named


def pack_kernel(group, experts, fold, routes_in, tokens_in, packed_ref, routes_ref, tokens_ref, sem):
    loads = [
        pltpu.make_async_copy(routes_in, routes_ref, sem.at[0]),
        pltpu.make_async_copy(tokens_in, tokens_ref, sem.at[1]),
    ]
    for load in loads:
        load.start()
    for load in loads:
        load.wait()
    count = 2 * packed_ref.shape[0]
    features = tokens_ref.shape[1]
    code = slot_codes(routed(routes_ref, experts)).astype(BF16)
    expert, first = message_rows(group, (count, 1), 0, fold)
    spread = jnp.where(expert == iota((count, experts), 1), 1.0, 0.0).astype(BF16)
    seen = dot(spread, code) - first.astype(F32)
    tokens = tokens_ref[...]
    for q in range(fold):
        placing = jnp.where(seen == q, 1.0, 0.0).astype(BF16)
        rows = dot(placing, tokens).astype(BF16).reshape(count // 2, 2, features)
        packed_ref[:, :, q * features : (q + 1) * features] = rows


def gate_kernel(group, experts, fold, routes_ref, gates_ref, weights_ref):
    top, rows = routes_ref.shape
    count = weights_ref.shape[2] // fold
    expert = iota((experts, rows), 0)
    gate = jnp.zeros((experts, rows), F32)
    for k in range(top):
        gate = gate + jnp.where(routes_ref[k : k + 1, :] == expert, gates_ref[k : k + 1, :], 0.0)
    code = slot_codes(routed(routes_ref, experts)).T.astype(BF16)
    gate = gate.T
    expert, first = message_rows(group, (1, count), 1, fold)
    spread = jnp.where(expert == iota((experts, count), 0), 1.0, 0.0).astype(BF16)
    seen = dot(code, spread) - first.astype(F32)
    for part in range(weights_ref.shape[0]):
        piece = gate.astype(BF16)
        gate = gate - piece.astype(F32)
        chosen = dot(piece, spread)
        for q in range(fold):
            weights_ref[part, :, q * count : (q + 1) * count] = jnp.where(
                seen == q, chosen, 0.0
            ).astype(BF16)


def up_kernel(fold, me_ref, arrived_ref, own_ref, *refs):
    others, out_ref, rows_ref = refs[:-2], refs[-2], refs[-1]
    side, _, features = rows_ref.shape
    each = arrived_ref.shape[0] // side
    tile = out_ref.shape[2]

    @pl.when(pl.program_id(0) == 0)
    def _():
        for s in range(side):
            for q in range(fold):
                rows_ref[s, q * each : (q + 1) * each, :] = arrived_ref[
                    s * each : (s + 1) * each, q * features : (q + 1) * features
                ]

    total = dot(rows_ref[me_ref[0]], own_ref[0])
    for k, w_ref in enumerate(others, 1):
        total = total + dot(rows_ref[lax.rem(me_ref[0] + side - k, side)], w_ref[...])
    for n in range(out_ref.shape[0]):
        out_ref[n] = total[:, n * tile : (n + 1) * tile].astype(BF16)


def hidden_kernel(share, parts_ref, out_ref):
    total = parts_ref[0].astype(F32)
    for n in range(1, parts_ref.shape[0]):
        total = total + parts_ref[n].astype(F32)
    width = total.shape[1]
    up = pltpu.roll(total, width - share, 1)
    mixed = (total / (1.0 + jnp.exp(-total)) * up).astype(BF16)
    column = iota((width, 1), 0)
    block = jnp.zeros_like(column)
    for n in range(1, width // (2 * share)):
        block = block + jnp.where(column >= 2 * share * n, 1, 0)
    unit = jnp.where(column - 2 * share * block < share, column - share * block, -width)
    lane = iota((width, width), 1)
    left = jnp.where(unit == lane, 1.0, 0.0).astype(BF16)
    right = jnp.where(unit + width // 2 == lane, 1.0, 0.0).astype(BF16)
    half = total.shape[0] // 2
    hidden = (dot(mixed[:half], left) + dot(mixed[half:], right)).astype(BF16)
    for n in range(out_ref.shape[0]):
        out_ref[n] = hidden


def down_kernel(batches, fold, me_ref, hidden_ref, own_ref, *refs):
    others, out_ref = refs[:-1], refs[-1]
    side, packed, width = hidden_ref.shape
    each = out_ref.shape[0] // side
    features = out_ref.shape[2] // fold
    half = packed // batches
    left = jnp.concatenate([hidden_ref[b, :, : width // 2] for b in range(side)], axis=1)
    right = jnp.concatenate([hidden_ref[b, :, width // 2 :] for b in range(side)], axis=1)
    pieces = []
    for n in range(batches):
        pieces += [left[n * half : (n + 1) * half], right[n * half : (n + 1) * half]]
    hidden = jnp.concatenate(pieces, axis=0)
    for k in range(side):
        w = own_ref[0] if k == 0 else others[k - 1][...]
        made = dot(hidden, w).astype(BF16)
        place = lax.rem(me_ref[0] + side - k, side) if k else me_ref[0]
        for q in range(fold):
            rows = made[2 * q * each : 2 * (q + 1) * each].reshape(each, 2, features)
            out_ref[pl.ds(place * each, each), :, q * features : (q + 1) * features] = rows


def take_kernel(me_ref, weights_ref, out_ref):
    out_ref[...] = weights_ref[0]


def keep_kernel(*refs):
    sem = refs[-1]
    parts, outs = refs[: len(refs) // 2], refs[len(refs) // 2 : -1]
    copies = [pltpu.make_async_copy(p, o, sem.at[n]) for n, (p, o) in enumerate(zip(parts, outs))]
    for copy in copies:
        copy.start()
    for copy in copies:
        copy.wait()


def mix_kernel(fold, tokens_ref, weights_ref, home_ref, out_ref):
    features = tokens_ref.shape[1]
    home = jnp.concatenate(
        [home_ref[:, q * features : (q + 1) * features] for q in range(fold)], axis=0
    )
    total = tokens_ref[...].astype(F32)
    for part in range(weights_ref.shape[0]):
        total = total + dot(weights_ref[part], home)
    out_ref[...] = total.astype(BF16)


def params(*semantics):
    return pltpu.CompilerParams(
        dimension_semantics=semantics or None, vmem_limit_bytes=VMEM_LIMIT
    )


def cost(flops, nbytes):
    return pl.CostEstimate(flops=flops, bytes_accessed=nbytes, transcendentals=0)


def per_device(mesh_shape, tokens, routes, gates, w_gate_up, w_down):
    rows, features = tokens.shape
    outer, inner = mesh_shape
    group, _, columns = w_gate_up.shape
    hidden = w_down.shape[1]
    experts = group * outer
    cap = 10
    slots = experts * cap
    per_expert = outer * cap
    side = group
    fold = cap // 2
    count = 2 * experts
    across = [[y * side + x for x in range(side)] for y in range(side)]
    along = [[y * side + x for y in range(side)] for x in range(side)]
    column = [[o * inner + n for n in line for o in range(outer)] for line in along]
    me = lax.axis_index("inner") // side
    me_ref = me.astype(jnp.int32).reshape(1)
    hbm = pl.BlockSpec(memory_space=pltpu.HBM)
    in_hbm = functools.partial(pltpu.with_memory_space_constraint, memory_space=pltpu.HBM)

    def exchange(value, axes, groups):
        return lax.all_to_all(
            value, axes, split_axis=0, concat_axis=0, tiled=True, axis_index_groups=groups
        )

    def to_column(messages):
        messages = messages.reshape(experts, 2, fold * features)
        got = exchange(messages, ("outer", "inner"), column)
        return got.reshape(count, fold * features)

    def take(weights, k):
        _, *share = weights.shape
        return pl.pallas_call(
            take_kernel,
            grid_spec=pltpu.PrefetchScalarGridSpec(
                num_scalar_prefetch=1,
                grid=(1,),
                in_specs=[pl.BlockSpec((1, *share), lambda n, me: (lax.rem(me[0] + k, side), 0, 0))],
                out_specs=pl.BlockSpec(share, lambda n, me: (0, 0)),
            ),
            out_shape=pltpu.HBM(share, BF16),
            compiler_params=params("arbitrary"),
            cost_estimate=cost(1, 4 * share[0] * share[1]),
            name="take",
        )(me_ref, in_hbm(weights))

    def from_line(weights, k, taken=None):
        pairs = [(line[n], line[(n + k) % side]) for line in along for n in range(side)]
        if taken is None:
            taken = lax.dynamic_index_in_dim(weights, (me + k) % side, 0, keepdims=False)
        return lax.ppermute(taken, "inner", pairs)

    def keep(parts, weight, name):
        return pl.pallas_call(
            keep_kernel,
            in_specs=[pl.BlockSpec(memory_space=pltpu.VMEM)] * len(parts),
            out_specs=[pl.BlockSpec(memory_space=pltpu.HBM)] * len(parts),
            out_shape=[pltpu.HBM(part.shape, BF16) for part in parts],
            scratch_shapes=[pltpu.SemaphoreType.DMA((len(parts),))],
            compiler_params=params(),
            cost_estimate=cost(weight, 4 * len(parts) * parts[0].size),
            name=name,
        )(*parts)

    (far,) = keep([from_line(w_gate_up, 2)], 20000000000, "keep_up")
    routes, gates = routes.T, gates.T

    packed = pl.pallas_call(
        functools.partial(pack_kernel, group, experts, fold),
        in_specs=[hbm, hbm],
        out_specs=pl.BlockSpec(memory_space=pltpu.VMEM),
        scratch_shapes=[
            pltpu.VMEM(routes.shape, routes.dtype),
            pltpu.VMEM(tokens.shape, tokens.dtype),
            pltpu.SemaphoreType.DMA((2,)),
        ],
        out_shape=jax.ShapeDtypeStruct((experts, 2, fold * features), BF16),
        compiler_params=params(),
        cost_estimate=cost(4 * slots * rows * features, 2 * slots * features),
        name="pack",
    )(in_hbm(routes), in_hbm(tokens))
    packed, up_late, down_late = lax.optimization_barrier((packed, w_gate_up, w_down))
    arrived = to_column(packed)
    near = [from_line(up_late, k, take(up_late, k)) for k in (1, 3)]
    up_weights = [near[0], far, near[1]]
    up_weights = [in_hbm(part) for part in up_weights]
    down_weights = keep([from_line(down_late, k) for k in range(1, side)], 20000000000, "keep_down")

    tile = columns // side
    partial_value = pl.pallas_call(
        functools.partial(up_kernel, fold),
        grid_spec=pltpu.PrefetchScalarGridSpec(
            num_scalar_prefetch=1,
            grid=(side // 2,),
            in_specs=[
                pl.BlockSpec((count, fold * features), lambda c, me: (0, 0)),
                pl.BlockSpec((1, features, 2 * tile), lambda c, me: (me[0], 0, c)),
            ]
            + [pl.BlockSpec((features, 2 * tile), lambda c, me: (0, c))] * (side - 1),
            out_specs=pl.BlockSpec((2, per_expert, tile), lambda c, me: (c, 0, 0)),
            scratch_shapes=[pltpu.VMEM((side, per_expert, features), BF16)],
        ),
        out_shape=jax.ShapeDtypeStruct((side, per_expert, tile), BF16),
        compiler_params=params("arbitrary"),
        cost_estimate=cost(2 * slots * features * columns, 8 * features * columns),
        name="gate_up",
    )(me_ref, arrived, in_hbm(w_gate_up), *up_weights)
    swapped = exchange(partial_value.reshape(side * per_expert, tile), "inner", across)
    swapped, *down_weights = lax.optimization_barrier((swapped, *down_weights))
    batches = 2
    packed_rows = per_expert // 2
    mine = pl.pallas_call(
        functools.partial(hidden_kernel, hidden // inner),
        grid=(batches,),
        in_specs=[pl.BlockSpec((side, per_expert // batches, tile), lambda n: (0, n, 0))],
        out_specs=pl.BlockSpec((side, packed_rows // batches, tile), lambda n: (0, n, 0)),
        out_shape=jax.ShapeDtypeStruct((side, packed_rows, tile), BF16),
        compiler_params=params("arbitrary"),
        cost_estimate=cost(per_expert * tile * tile, 4 * per_expert * tile * side),
        name="hidden",
    )(swapped.reshape(side, per_expert, tile))
    gathered = exchange(mine.reshape(side * packed_rows, tile), "inner", across)
    expert_out = pl.pallas_call(
        functools.partial(down_kernel, batches, fold),
        grid_spec=pltpu.PrefetchScalarGridSpec(
            num_scalar_prefetch=1,
            grid=(1,),
            in_specs=[
                pl.BlockSpec((side, packed_rows, tile), lambda n, me: (0, 0, 0)),
                pl.BlockSpec((1, hidden, features), lambda n, me: (me[0], 0, 0)),
            ]
            + [pl.BlockSpec((hidden, features), lambda n, me: (0, 0))] * (side - 1),
            out_specs=pl.BlockSpec((experts, 2, fold * features), lambda n, me: (0, 0, 0)),
        ),
        out_shape=jax.ShapeDtypeStruct((experts, 2, fold * features), BF16),
        compiler_params=params("arbitrary"),
        cost_estimate=cost(2 * slots * features * hidden, 8 * features * hidden),
        name="down",
    )(me_ref, gathered.reshape(side, packed_rows, tile), in_hbm(w_down), *map(in_hbm, down_weights))
    weights = pl.pallas_call(
        functools.partial(gate_kernel, group, experts, fold),
        out_shape=jax.ShapeDtypeStruct((3, rows, slots), BF16),
        compiler_params=params(),
        cost_estimate=cost(2 * rows * experts * slots, 6 * rows * slots),
        name="gate_weights",
    )(routes, gates)
    home = to_column(expert_out)
    return pl.pallas_call(
        functools.partial(mix_kernel, fold),
        out_shape=jax.ShapeDtypeStruct((rows, features), BF16),
        compiler_params=params(),
        cost_estimate=cost(6 * rows * slots * features, 2 * slots * features),
        name="mix",
    )(tokens, weights, home)


def solution(mesh):
    in_specs = (
        P("outer", "inner"),
        P("outer", None),
        P("outer", None),
        P("outer", "inner", None),
        P("outer", None, "inner"),
    )
    return jax.shard_map(
        functools.partial(per_device, (mesh.shape["outer"], mesh.shape["inner"])),
        mesh=mesh,
        in_specs=in_specs,
        out_specs=P("outer", "inner"),
        check_vma=False,
    )
```
